256 devices in a mesh: blk: 256 (over y, x, z, core).
Axes of the slice: x: 4, y: 4, z: 8, core: 2. Of those that a mesh axis runs over, the one named last changes fastest.
Arguments:
- integrals: float32 [131072, 2176], P('blk'), may hold values from -0.125 to 0.125
- tile_pattern: int32 [1024, 17], P('blk'), may hold values 0 or 1
- amplitudes: float32 [131072, 1280], P('blk'), may hold values from -6 to 6
- residual_in: float32 [131072, 1280], P('blk'), may hold values from -6 to 6
Outputs:
- residual: float32 [131072, 1280], P('blk')
The draws below stay inside these ranges and needn't reach their ends.
Inputs may be any that keep to these rules, and one draw needn't show every extreme that they name: `tile_pattern`: 1 where the integral tile is significant, 0 where it is neglected.
All inputs are finite; a program needn't handle non-finite values. No bound on the sum of `tile_pattern` on one device may be relied on, other than what follows from the above.
Results may differ from the reference program's by a relative error of at most 0.0003.
Values sent between devices are 32-bit elements; how exact they have to be, the bound alone decides.
No kernel may reach another device: no remote copies, remote signals or barrier semaphores. Data moves between devices by JAX's collectives and lax.ppermute only.
A program may use at most 64 MiB of HBM per device.

```python
import jax
import jax.numpy as jnp
from jax import lax

TB = 128
W = 8
NIJ = 1280
NT = 1024
NAB = 131072


def set_ends(drawn, own_key, low, largest):
    dims = drawn.shape
    spot = [jax.random.randint(jax.random.fold_in(own_key, axis), (), 0, dims[axis]) for axis in range(len(dims))]
    drawn = drawn.at[tuple(spot)].set(low)
    longest = dims.index(max(dims))
    spot[longest] = (spot[longest] + 1) % dims[longest]
    return drawn.at[tuple(spot)].set(largest)


def levels(stream_key, extent, cuts, low, top_value):
    loudness, own = 1.0, jax.random.fold_in(stream_key, 6)
    for dim, blocks in cuts:
        heights = jnp.exp(jax.random.uniform(jax.random.fold_in(own, dim), (blocks,), jnp.float32, low / len(cuts), top_value / len(cuts)))
        loudness = loudness * jnp.repeat(heights, extent[dim] // blocks).reshape([-1 if axis == dim else 1 for axis in range(len(extent))])
    return loudness


def centred(rng, shape, scale, limit, cuts=(), kind=jnp.bfloat16):
    values = scale * jax.random.normal(rng, shape, jnp.float32)
    if cuts:
        values = values * levels(rng, shape, cuts, -0.22, 0.18)
    return jnp.clip(values, -limit, limit).astype(kind)


def setup_inputs(seed: int = 0) -> dict:
    keys = jax.random.split(jax.random.key(seed), 5)
    return {
        "integrals": centred(keys[0], (NAB, (2 * W + 1) * TB), ((2 * W + 1) * TB) ** -0.5, 0.125, ((0, 256),), jnp.float32),
        "tile_pattern": set_ends((jax.random.randint(keys[1], (NT, 2 * W + 1), 0, 4) < 3).astype(jnp.int32), jax.random.fold_in(keys[1], 1), 0, 1),
        "amplitudes": centred(keys[2], (NAB, NIJ), 1.0, 6.0, ((0, 256),), jnp.float32),
        "residual_in": centred(keys[3], (NAB, NIJ), 1.0, 6.0, ((0, 256),), jnp.float32),
    }


def reference(integrals, tile_pattern, amplitudes, residual_in):
    band = 2 * W + 1
    mask = jnp.repeat(tile_pattern.astype(jnp.float32), TB, axis=1)
    masked = integrals.reshape(NT, TB, band * TB) * mask[:, None, :]
    extended = jnp.concatenate([amplitudes[NAB - W * TB:], amplitudes, amplitudes[:W * TB]], 0)

    def one_tile(tile_row):
        rows = lax.dynamic_slice_in_dim(extended, (tile_row * TB).astype(jnp.int32), band * TB, 0)
        return jnp.dot(masked[tile_row], rows, precision=lax.Precision.HIGHEST, preferred_element_type=jnp.float32)

    ladder = lax.map(one_tile, jnp.arange(NT, dtype=jnp.int32)).reshape(NAB, NIJ)
    return residual_in + ladder
```

```python
import functools

import jax
import jax.numpy as jnp
from jax import lax
from jax.experimental import pallas as pl
from jax.experimental.pallas import tpu as pltpu
from jax.sharding import PartitionSpec as P

TB = 128
W = 8
BAND = 2 * W + 1
AXIS = "blk"

OWN, PARTNER, FACING, BESIDE, BEYOND = range(5)


def exchange(value, offset):
    count = lax.axis_size(AXIS)
    pairs = []
    for low in range(offset, count + offset, 2):
        a, b = low % count, (low + 1) % count
        pairs += [(a, b), (b, a)]
    return lax.ppermute(value, AXIS, pairs)


def split(x):
    high = x.astype(jnp.bfloat16)
    low = (x - high.astype(jnp.float32)).astype(jnp.bfloat16)
    return high, low


def align_kernel(tiles, pattern_ref, v_ref, high_ref, low_ref):
    row = pl.program_id(0)
    odd = lax.rem(lax.axis_index(AXIS), 2)
    sign = 1 - 2 * odd
    for role, step in ((OWN, 0), (PARTNER, 1), (FACING, -1), (BESIDE, 2), (BEYOND, -2)):
        block = 2 + sign * step
        for t in range(tiles):
            k = block * tiles + t - row
            inside = jnp.logical_and(k >= 0, k < BAND)
            k = jnp.clip(k, 0, BAND - 1)
            keep = jnp.where(inside, pattern_ref[row, k], 0).astype(jnp.float32)
            tile = v_ref[:, pl.ds(pl.multiple_of(k * TB, TB), TB)] * keep
            high, low = split(tile)
            high_ref[role, :, t * TB : (t + 1) * TB] = high
            low_ref[role, :, t * TB : (t + 1) * TB] = low


def align(integrals, tile_pattern):
    rows = integrals.shape[0]
    tiles = rows // TB
    shape = jax.ShapeDtypeStruct((5, rows, rows), jnp.bfloat16)
    spec = pl.BlockSpec((5, TB, rows), lambda r: (0, r, 0))
    return pl.pallas_call(
        functools.partial(align_kernel, tiles),
        grid=(tiles,),
        in_specs=[
            pl.BlockSpec(memory_space=pltpu.SMEM),
            pl.BlockSpec((TB, BAND * TB), lambda r: (r, 0)),
        ],
        out_specs=[spec, spec],
        out_shape=[shape, shape],
        compiler_params=pltpu.CompilerParams(vmem_limit_bytes=24 * 2**20),
        cost_estimate=pl.CostEstimate(flops=10 * rows * rows, bytes_accessed=10**7, transcendentals=0),
        name="align",
    )(tile_pattern, integrals)


def add_kernel(count, *refs):
    *blocks, acc_ref, out_ref = refs
    total = acc_ref[...]
    for i in range(count):
        vh_ref, vl_ref, t_ref = blocks[3 * i : 3 * i + 3]
        th, tl = split(t_ref[...])
        vh, vl = vh_ref[0], vl_ref[0]
        dot = functools.partial(jnp.dot, preferred_element_type=jnp.float32)
        total += dot(vh, th) + (dot(vh, tl) + dot(vl, th))
    out_ref[...] = total


def add_products(acc, high, low, parts, cols, name):
    rows, width = acc.shape
    args, specs = [], []
    for role, piece, block in parts:
        deep = block.shape[0]
        spec = pl.BlockSpec((1, rows, deep), lambda j, role=role, piece=piece: (role, 0, piece))
        args += [high, low, block]
        specs += [spec, spec, pl.BlockSpec((deep, cols), lambda j: (0, j))]
    args.append(acc)
    specs.append(pl.BlockSpec((rows, cols), lambda j: (0, j)))
    n = len(parts)
    return pl.pallas_call(
        functools.partial(add_kernel, n),
        grid=(width // cols,),
        in_specs=specs,
        out_specs=pl.BlockSpec((rows, cols), lambda j: (0, j)),
        out_shape=jax.ShapeDtypeStruct(acc.shape, acc.dtype),
        compiler_params=pltpu.CompilerParams(vmem_limit_bytes=32 * 2**20),
        cost_estimate=pl.CostEstimate(flops=1, bytes_accessed=1, transcendentals=0),
        name=name,
    )(*args)


def last_kernel(start, step, *refs):
    high_ref, low_ref, block_ref, acc_ref = refs[:4]
    out_ref, stage, sems = refs[-3:]
    copies = []
    for i in range(block_ref.shape[1] // step):
        here = slice(i * step, i * step + step)
        there = slice(start + i * step, start + i * step + step)
        th, tl = split(block_ref[:, here])
        vh, vl = high_ref[BEYOND], low_ref[BEYOND]
        dot = functools.partial(jnp.dot, preferred_element_type=jnp.float32)
        stage[:, here] = acc_ref[:, there] + (dot(vh, th) + (dot(vh, tl) + dot(vl, th)))
        copies.append(pltpu.make_async_copy(stage.at[:, here], out_ref.at[:, there], sems.at[i]))
        copies[-1].start()
    for copy in copies:
        copy.wait()


def add_last(acc, high, low, block, start, out, name):
    rows, width = block.shape
    step = 256
    args = [high, low, block, acc]
    specs = [pl.BlockSpec(memory_space=pltpu.VMEM)] * 4
    aliases = {}
    if out is not None:
        aliases = {len(args): 0}
        args.append(out)
        specs.append(pl.BlockSpec(memory_space=pl.ANY))
    return pl.pallas_call(
        functools.partial(last_kernel, start, step),
        in_specs=specs,
        out_specs=pl.BlockSpec(memory_space=pl.ANY),
        out_shape=jax.ShapeDtypeStruct(acc.shape, acc.dtype),
        input_output_aliases=aliases,
        scratch_shapes=[pltpu.VMEM((rows, width), jnp.float32), pltpu.SemaphoreType.DMA((width // step,))],
        compiler_params=pltpu.CompilerParams(vmem_limit_bytes=16 * 2**20),
        cost_estimate=pl.CostEstimate(flops=1, bytes_accessed=1, transcendentals=0),
        name=name,
    )(*args)


def per_device(integrals, tile_pattern, amplitudes, residual_in):
    rows, width = amplitudes.shape
    facing = exchange(amplitudes, 1)
    high, low = align(integrals, tile_pattern)
    partner = exchange(amplitudes, 0)
    cuts = [0, 768, 1280]
    beyond = [exchange(partner[:, a:b], 1) for a, b in zip(cuts, cuts[1:])]
    acc = add_products(residual_in, high, low, [(OWN, 0, amplitudes), (PARTNER, 0, partner)], 256, "near")
    facing, acc = lax.optimization_barrier((facing, acc))
    n = rows // 4
    beside = [exchange(facing[i : i + n], 0) for i in range(0, rows, n)]
    parts = [(FACING, 0, facing)] + [(BESIDE, i, block) for i, block in enumerate(beside)]
    acc = add_products(acc, high, low, parts, 256, "middle")
    out = None
    for i, block in enumerate(beyond):
        out = add_last(acc, high, low, block, cuts[i], out, "last%d" % i)
    return out


def solution(mesh):
    return jax.shard_map(
        per_device,
        mesh=mesh,
        in_specs=(P("blk", None), P("blk", None), P("blk", None), P("blk", None)),
        out_specs=P("blk", None),
        check_vma=False,
    )
```

```python
import functools

import jax
import jax.numpy as jnp
from jax import lax
from jax.experimental import pallas as pl
from jax.experimental.pallas import tpu as pltpu
from jax.sharding import PartitionSpec as P

TB = 128
W = 8
BAND = 2 * W + 1
AXIS = "blk"

OWN, PARTNER, FACING, BESIDE, BEYOND = range(5)


def exchange(value, offset):
    count = lax.axis_size(AXIS)
    pairs = []
    for low in range(offset, count + offset, 2):
        a, b = low % count, (low + 1) % count
        pairs += [(a, b), (b, a)]
    return lax.ppermute(value, AXIS, pairs)


def split(x):
    high = x.astype(jnp.bfloat16)
    low = (x - high.astype(jnp.float32)).astype(jnp.bfloat16)
    return high, low


def align_kernel(tiles, pattern_ref, v_ref, high_ref, low_ref):
    row = pl.program_id(0)
    odd = lax.rem(lax.axis_index(AXIS), 2)
    sign = 1 - 2 * odd
    for role, step in ((OWN, 0), (PARTNER, 1), (FACING, -1), (BESIDE, 2), (BEYOND, -2)):
        block = 2 + sign * step
        for t in range(tiles):
            k = block * tiles + t - row
            inside = jnp.logical_and(k >= 0, k < BAND)
            k = jnp.clip(k, 0, BAND - 1)
            keep = jnp.where(inside, pattern_ref[row, k], 0).astype(jnp.float32)
            tile = v_ref[:, pl.ds(pl.multiple_of(k * TB, TB), TB)] * keep
            high, low = split(tile)
            high_ref[role, :, t * TB : (t + 1) * TB] = high
            low_ref[role, :, t * TB : (t + 1) * TB] = low


def align(integrals, tile_pattern):
    rows = integrals.shape[0]
    tiles = rows // TB
    shape = jax.ShapeDtypeStruct((5, rows, rows), jnp.bfloat16)
    spec = pl.BlockSpec((5, TB, rows), lambda r: (0, r, 0))
    return pl.pallas_call(
        functools.partial(align_kernel, tiles),
        grid=(tiles,),
        in_specs=[
            pl.BlockSpec(memory_space=pltpu.SMEM),
            pl.BlockSpec((TB, BAND * TB), lambda r: (r, 0)),
        ],
        out_specs=[spec, spec],
        out_shape=[shape, shape],
        compiler_params=pltpu.CompilerParams(vmem_limit_bytes=24 * 2**20),
        cost_estimate=pl.CostEstimate(flops=10 * rows * rows, bytes_accessed=10**7, transcendentals=0),
        name="align",
    )(tile_pattern, integrals)


def add_kernel(count, *refs):
    *blocks, acc_ref, out_ref = refs
    total = acc_ref[...]
    for i in range(count):
        vh_ref, vl_ref, t_ref = blocks[3 * i : 3 * i + 3]
        th, tl = split(t_ref[...])
        vh, vl = vh_ref[0], vl_ref[0]
        dot = functools.partial(jnp.dot, preferred_element_type=jnp.float32)
        total += dot(vh, th) + (dot(vh, tl) + dot(vl, th))
    out_ref[...] = total


def add_products(acc, high, low, parts, cols, name):
    rows, width = acc.shape
    args, specs = [], []
    for role, piece, block in parts:
        deep = block.shape[0]
        spec = pl.BlockSpec((1, rows, deep), lambda j, role=role, piece=piece: (role, 0, piece))
        args += [high, low, block]
        specs += [spec, spec, pl.BlockSpec((deep, cols), lambda j: (0, j))]
    args.append(acc)
    specs.append(pl.BlockSpec((rows, cols), lambda j: (0, j)))
    n = len(parts)
    return pl.pallas_call(
        functools.partial(add_kernel, n),
        grid=(width // cols,),
        in_specs=specs,
        out_specs=pl.BlockSpec((rows, cols), lambda j: (0, j)),
        out_shape=jax.ShapeDtypeStruct(acc.shape, acc.dtype),
        compiler_params=pltpu.CompilerParams(vmem_limit_bytes=32 * 2**20),
        cost_estimate=pl.CostEstimate(flops=1, bytes_accessed=1, transcendentals=0),
        name=name,
    )(*args)


def last_kernel(start, step, *refs):
    high_ref, low_ref, block_ref, acc_ref = refs[:4]
    out_ref, stage, sems = refs[-3:]
    copies = []
    for i in range(block_ref.shape[1] // step):
        here = slice(i * step, i * step + step)
        there = slice(start + i * step, start + i * step + step)
        th, tl = split(block_ref[:, here])
        vh, vl = high_ref[BEYOND], low_ref[BEYOND]
        dot = functools.partial(jnp.dot, preferred_element_type=jnp.float32)
        stage[:, here] = acc_ref[:, there] + (dot(vh, th) + (dot(vh, tl) + dot(vl, th)))
        copies.append(pltpu.make_async_copy(stage.at[:, here], out_ref.at[:, there], sems.at[i]))
        copies[-1].start()
    for copy in copies:
        copy.wait()


def add_last(acc, high, low, block, start, out, name):
    rows, width = block.shape
    step = 256
    args = [high, low, block, acc]
    specs = [pl.BlockSpec(memory_space=pltpu.VMEM)] * 4
    aliases = {}
    if out is not None:
        aliases = {len(args): 0}
        args.append(out)
        specs.append(pl.BlockSpec(memory_space=pl.ANY))
    return pl.pallas_call(
        functools.partial(last_kernel, start, step),
        in_specs=specs,
        out_specs=pl.BlockSpec(memory_space=pl.ANY),
        out_shape=jax.ShapeDtypeStruct(acc.shape, acc.dtype),
        input_output_aliases=aliases,
        scratch_shapes=[pltpu.VMEM((rows, width), jnp.float32), pltpu.SemaphoreType.DMA((width // step,))],
        compiler_params=pltpu.CompilerParams(vmem_limit_bytes=16 * 2**20),
        cost_estimate=pl.CostEstimate(flops=1, bytes_accessed=1, transcendentals=0),
        name=name,
    )(*args)


def per_device(integrals, tile_pattern, amplitudes, residual_in):
    rows, width = amplitudes.shape
    facing = exchange(amplitudes, 1)
    high, low = align(integrals, tile_pattern)
    n = rows // 2
    pieces = [exchange(amplitudes[i : i + n], 0) for i in range(0, rows, n)]
    partner = jnp.concatenate(pieces, 0)
    cuts = [0, 1024, 1280]
    beyond = [exchange(partner[:, a:b], 1) for a, b in zip(cuts, cuts[1:])]
    acc = add_products(residual_in, high, low, [(OWN, 0, amplitudes), (PARTNER, 0, partner)], 256, "near")
    facing, acc = lax.optimization_barrier((facing, acc))
    n = rows // 2
    beside = [exchange(facing[i : i + n], 0) for i in range(0, rows, n)]
    parts = [(FACING, 0, facing), (BESIDE, 0, jnp.concatenate(beside, 0))]
    acc = add_products(acc, high, low, parts, 256, "middle")
    out = None
    for i, block in enumerate(beyond):
        out = add_last(acc, high, low, block, cuts[i], out, "last%d" % i)
    return out


def solution(mesh):
    return jax.shard_map(
        per_device,
        mesh=mesh,
        in_specs=(P("blk", None), P("blk", None), P("blk", None), P("blk", None)),
        out_specs=P("blk", None),
        check_vma=False,
    )
```

```python
import functools

import jax
import jax.numpy as jnp
from jax import lax
from jax.experimental import pallas as pl
from jax.experimental.pallas import tpu as pltpu
from jax.sharding import PartitionSpec as P

TB = 128
W = 8
BAND = 2 * W + 1
AXIS = "blk"

OWN, PARTNER, FACING, BESIDE, BEYOND = range(5)


def exchange(value, offset):
    count = lax.axis_size(AXIS)
    pairs = []
    for low in range(offset, count + offset, 2):
        a, b = low % count, (low + 1) % count
        pairs += [(a, b), (b, a)]
    return lax.ppermute(value, AXIS, pairs)


def split(x):
    high = x.astype(jnp.bfloat16)
    low = (x - high.astype(jnp.float32)).astype(jnp.bfloat16)
    return high, low


def align_kernel(tiles, pattern_ref, v_ref, high_ref, low_ref):
    row = pl.program_id(0)
    odd = lax.rem(lax.axis_index(AXIS), 2)
    sign = 1 - 2 * odd
    for role, step in ((OWN, 0), (PARTNER, 1), (FACING, -1), (BESIDE, 2), (BEYOND, -2)):
        block = 2 + sign * step
        for t in range(tiles):
            k = block * tiles + t - row
            inside = jnp.logical_and(k >= 0, k < BAND)
            k = jnp.clip(k, 0, BAND - 1)
            keep = jnp.where(inside, pattern_ref[row, k], 0).astype(jnp.float32)
            tile = v_ref[:, pl.ds(pl.multiple_of(k * TB, TB), TB)] * keep
            high, low = split(tile)
            high_ref[role, :, t * TB : (t + 1) * TB] = high
            low_ref[role, :, t * TB : (t + 1) * TB] = low


def align(integrals, tile_pattern):
    rows = integrals.shape[0]
    tiles = rows // TB
    shape = jax.ShapeDtypeStruct((5, rows, rows), jnp.bfloat16)
    spec = pl.BlockSpec((5, TB, rows), lambda r: (0, r, 0))
    return pl.pallas_call(
        functools.partial(align_kernel, tiles),
        grid=(tiles,),
        in_specs=[
            pl.BlockSpec(memory_space=pltpu.SMEM),
            pl.BlockSpec((TB, BAND * TB), lambda r: (r, 0)),
        ],
        out_specs=[spec, spec],
        out_shape=[shape, shape],
        compiler_params=pltpu.CompilerParams(vmem_limit_bytes=24 * 2**20),
        cost_estimate=pl.CostEstimate(flops=10 * rows * rows, bytes_accessed=10**7, transcendentals=0),
        name="align",
    )(tile_pattern, integrals)


def add_kernel(count, *refs):
    *blocks, acc_ref, out_ref = refs
    total = acc_ref[...]
    for i in range(count):
        vh_ref, vl_ref, t_ref = blocks[3 * i : 3 * i + 3]
        th, tl = split(t_ref[...])
        vh, vl = vh_ref[0], vl_ref[0]
        dot = functools.partial(jnp.dot, preferred_element_type=jnp.float32)
        total += dot(vh, th) + (dot(vh, tl) + dot(vl, th))
    out_ref[...] = total


def add_products(acc, high, low, parts, cols, name):
    rows, width = acc.shape
    args, specs = [], []
    for role, piece, block in parts:
        deep = block.shape[0]
        spec = pl.BlockSpec((1, rows, deep), lambda j, role=role, piece=piece: (role, 0, piece))
        args += [high, low, block]
        specs += [spec, spec, pl.BlockSpec((deep, cols), lambda j: (0, j))]
    args.append(acc)
    specs.append(pl.BlockSpec((rows, cols), lambda j: (0, j)))
    n = len(parts)
    return pl.pallas_call(
        functools.partial(add_kernel, n),
        grid=(width // cols,),
        in_specs=specs,
        out_specs=pl.BlockSpec((rows, cols), lambda j: (0, j)),
        out_shape=jax.ShapeDtypeStruct(acc.shape, acc.dtype),
        compiler_params=pltpu.CompilerParams(vmem_limit_bytes=32 * 2**20),
        cost_estimate=pl.CostEstimate(flops=1, bytes_accessed=1, transcendentals=0),
        name=name,
    )(*args)


def last_kernel(start, step, count, *refs):
    high_ref, low_ref, acc_ref = refs[:3]
    block_refs = refs[3 : 3 + count]
    out_ref, stage, sems = refs[-3:]
    copies = []
    for i in range(stage.shape[1] // step):
        here = slice(i * step, i * step + step)
        there = slice(start + i * step, start + i * step + step)
        block = [ref[:, here] for ref in block_refs]
        if count == 3:
            block = [jnp.concatenate([block[0], block[1] + block[2]], 0)]
        th, tl = split(block[0])
        vh, vl = high_ref[BEYOND], low_ref[BEYOND]
        dot = functools.partial(jnp.dot, preferred_element_type=jnp.float32)
        stage[:, here] = acc_ref[:, there] + (dot(vh, th) + (dot(vh, tl) + dot(vl, th)))
        copies.append(pltpu.make_async_copy(stage.at[:, here], out_ref.at[:, there], sems.at[i]))
        copies[-1].start()
    for copy in copies:
        copy.wait()


def add_last(acc, high, low, blocks, start, out, name):
    rows, width = acc.shape[0], blocks[0].shape[1]
    step = 256
    args = [high, low, acc, *blocks]
    specs = [pl.BlockSpec(memory_space=pltpu.VMEM)] * len(args)
    aliases = {}
    if out is not None:
        aliases = {len(args): 0}
        args.append(out)
        specs.append(pl.BlockSpec(memory_space=pl.ANY))
    return pl.pallas_call(
        functools.partial(last_kernel, start, step, len(blocks)),
        in_specs=specs,
        out_specs=pl.BlockSpec(memory_space=pl.ANY),
        out_shape=jax.ShapeDtypeStruct(acc.shape, acc.dtype),
        input_output_aliases=aliases,
        scratch_shapes=[pltpu.VMEM((rows, width), jnp.float32), pltpu.SemaphoreType.DMA((width // step,))],
        compiler_params=pltpu.CompilerParams(vmem_limit_bytes=16 * 2**20),
        cost_estimate=pl.CostEstimate(flops=1, bytes_accessed=1, transcendentals=0),
        name=name,
    )(*args)


def hops(count):
    facing = [(i, (i + 1 if i % 2 else i - 1) % count) for i in range(count)]
    far = [pair for pair in facing if {i // 64 for i in pair} != {pair[0] // 64}]
    return facing, far


def per_device(integrals, tile_pattern, amplitudes, residual_in):
    rows, width = amplitudes.shape
    count = lax.axis_size(AXIS)
    pairs, far = hops(count)
    near = [pair for pair in pairs if pair not in far]
    cut, kept = 1024, rows - 128
    facing = exchange(amplitudes, 1)
    high, low = align(integrals, tile_pattern)
    n = rows // 2
    pieces = [exchange(amplitudes[i : i + n], 0) for i in range(0, rows, n)]
    partner = jnp.concatenate(pieces, 0)
    most = exchange(partner[:, :cut], 1)
    rest = exchange(partner[:kept, cut:], 1)
    slab = lax.ppermute(partner[kept:, cut:], AXIS, near)
    out, back = [], []
    for source, target in far:
        holder = source ^ 1
        relay = (holder + 16 if source % 2 else holder - 16) % count
        out.append((holder, relay))
        back.append((relay, target))
    held = lax.ppermute(amplitudes[kept:, cut:], AXIS, out)
    relayed = lax.ppermute(held, AXIS, back)
    acc = add_products(residual_in, high, low, [(OWN, 0, amplitudes), (PARTNER, 0, partner)], 256, "near")
    facing, acc = lax.optimization_barrier((facing, acc))
    n = rows // 2
    beside = [exchange(facing[i : i + n], 0) for i in range(0, rows, n)]
    parts = [(FACING, 0, facing), (BESIDE, 0, jnp.concatenate(beside, 0))]
    acc = add_products(acc, high, low, parts, 256, "middle")
    result = add_last(acc, high, low, [most], 0, None, "last0")
    return add_last(acc, high, low, [rest, slab, relayed], cut, result, "last1")


def solution(mesh):
    return jax.shard_map(
        per_device,
        mesh=mesh,
        in_specs=(P("blk", None), P("blk", None), P("blk", None), P("blk", None)),
        out_specs=P("blk", None),
        check_vma=False,
    )
```

```python
import functools

import jax
import jax.numpy as jnp
from jax import lax
from jax.experimental import pallas as pl
from jax.experimental.pallas import tpu as pltpu
from jax.sharding import PartitionSpec as P

TB = 128
W = 8
BAND = 2 * W + 1
AXIS = "blk"

OWN, PARTNER, FACING, BESIDE, BEYOND = range(5)


def exchange(value, offset):
    count = lax.axis_size(AXIS)
    pairs = []
    for low in range(offset, count + offset, 2):
        a, b = low % count, (low + 1) % count
        pairs += [(a, b), (b, a)]
    return lax.ppermute(value, AXIS, pairs)


def split(x):
    high = x.astype(jnp.bfloat16)
    low = (x - high.astype(jnp.float32)).astype(jnp.bfloat16)
    return high, low


def align_kernel(tiles, pattern_ref, v_ref, high_ref, low_ref):
    row = pl.program_id(0)
    odd = lax.rem(lax.axis_index(AXIS), 2)
    sign = 1 - 2 * odd
    for role, step in ((OWN, 0), (PARTNER, 1), (FACING, -1), (BESIDE, 2), (BEYOND, -2)):
        block = 2 + sign * step
        for t in range(tiles):
            k = block * tiles + t - row
            inside = jnp.logical_and(k >= 0, k < BAND)
            k = jnp.clip(k, 0, BAND - 1)
            keep = jnp.where(inside, pattern_ref[row, k], 0).astype(jnp.float32)
            tile = v_ref[:, pl.ds(pl.multiple_of(k * TB, TB), TB)] * keep
            high, low = split(tile)
            high_ref[role, :, t * TB : (t + 1) * TB] = high
            low_ref[role, :, t * TB : (t + 1) * TB] = low


def align(integrals, tile_pattern):
    rows = integrals.shape[0]
    tiles = rows // TB
    shape = jax.ShapeDtypeStruct((5, rows, rows), jnp.bfloat16)
    spec = pl.BlockSpec((5, TB, rows), lambda r: (0, r, 0))
    return pl.pallas_call(
        functools.partial(align_kernel, tiles),
        grid=(tiles,),
        in_specs=[
            pl.BlockSpec(memory_space=pltpu.SMEM),
            pl.BlockSpec((TB, BAND * TB), lambda r: (r, 0)),
        ],
        out_specs=[spec, spec],
        out_shape=[shape, shape],
        compiler_params=pltpu.CompilerParams(vmem_limit_bytes=24 * 2**20),
        cost_estimate=pl.CostEstimate(flops=10 * rows * rows, bytes_accessed=10**7, transcendentals=0),
        name="align",
    )(tile_pattern, integrals)


def product(vh_ref, vl_ref, t_ref):
    th, tl = split(t_ref[...])
    vh, vl = vh_ref[0], vl_ref[0]
    dot = functools.partial(jnp.dot, preferred_element_type=jnp.float32)
    return dot(vh, th) + (dot(vh, tl) + dot(vl, th))


def add_kernel(count, *refs):
    *blocks, acc_ref, out_ref = refs
    total = acc_ref[...]
    for i in range(count):
        total += product(*blocks[3 * i : 3 * i + 3])
    out_ref[...] = total
    if len(blocks) > 3 * count:

        @pl.when(pl.program_id(0) == pl.num_programs(0) - 1)
        def _():
            out_ref[...] += product(*blocks[3 * count :])


def add_products(acc, high, low, parts, cols, name, flops, edge=()):
    rows, width = acc.shape
    args, specs = [], []
    for role, piece, block in parts:
        deep = block.shape[0]
        spec = pl.BlockSpec((1, rows, deep), lambda j, role=role, piece=piece: (role, 0, piece))
        args += [high, low, block]
        specs += [spec, spec, pl.BlockSpec((deep, cols), lambda j: (0, j))]
    for role, piece, block in edge:
        deep = block.shape[0]
        spec = pl.BlockSpec((1, rows, deep), lambda j, role=role, piece=piece: (role, 0, piece))
        args += [high, low, block]
        specs += [spec, spec, pl.BlockSpec((deep, cols), lambda j: (0, 0))]
    args.append(acc)
    specs.append(pl.BlockSpec((rows, cols), lambda j: (0, j)))
    n = len(parts)
    return pl.pallas_call(
        functools.partial(add_kernel, n),
        grid=(width // cols,),
        in_specs=specs,
        out_specs=pl.BlockSpec((rows, cols), lambda j: (0, j)),
        out_shape=jax.ShapeDtypeStruct(acc.shape, acc.dtype),
        compiler_params=pltpu.CompilerParams(vmem_limit_bytes=32 * 2**20),
        cost_estimate=pl.CostEstimate(flops=flops, bytes_accessed=1, transcendentals=0),
        name=name,
    )(*args)


def last_kernel(start, step, count, *refs):
    high_ref, low_ref, acc_ref = refs[:3]
    block_refs = refs[3 : 3 + count]
    out_ref, stage, sems = refs[-3:]
    copies = []
    for i in range(stage.shape[1] // step):
        here = slice(i * step, i * step + step)
        there = slice(start + i * step, start + i * step + step)
        th, tl = split(jnp.concatenate([ref[:, here] for ref in block_refs], 0))
        vh, vl = high_ref[BEYOND], low_ref[BEYOND]
        dot = functools.partial(jnp.dot, preferred_element_type=jnp.float32)
        stage[:, here] = acc_ref[:, there] + (dot(vh, th) + (dot(vh, tl) + dot(vl, th)))
        copies.append(pltpu.make_async_copy(stage.at[:, here], out_ref.at[:, there], sems.at[i]))
        copies[-1].start()
    for copy in copies:
        copy.wait()


def add_last(acc, high, low, blocks, start, out, name):
    rows, width = acc.shape[0], blocks[0].shape[1]
    step = 256
    args = [high, low, acc, *blocks]
    specs = [pl.BlockSpec(memory_space=pltpu.VMEM)] * len(args)
    aliases = {}
    if out is not None:
        aliases = {len(args): 0}
        args.append(out)
        specs.append(pl.BlockSpec(memory_space=pl.ANY))
    return pl.pallas_call(
        functools.partial(last_kernel, start, step, len(blocks)),
        in_specs=specs,
        out_specs=pl.BlockSpec(memory_space=pl.ANY),
        out_shape=jax.ShapeDtypeStruct(acc.shape, acc.dtype),
        input_output_aliases=aliases,
        scratch_shapes=[pltpu.VMEM((rows, width), jnp.float32), pltpu.SemaphoreType.DMA((width // step,))],
        compiler_params=pltpu.CompilerParams(vmem_limit_bytes=16 * 2**20),
        cost_estimate=pl.CostEstimate(flops=1, bytes_accessed=1, transcendentals=0),
        name=name,
    )(*args)


def around(value):
    count = lax.axis_size(AXIS)
    routes = []
    for b in range(0, count, 16):
        routes.append([i % count for i in (b - 1, b + 9, b + 3, b)])
        routes.append([i % count for i in (b, b - 10, b - 4, b - 1)])
    for hop in range(3):
        value = lax.ppermute(value, AXIS, [(route[hop], route[hop + 1]) for route in routes])
    return value


def inside(value):
    count = lax.axis_size(AXIS)
    pairs = [(i, i + 1 if i % 2 else i - 1) for i in range(count) if i % 16 not in (0, 15)]
    return lax.ppermute(value, AXIS, pairs)


def per_device(integrals, tile_pattern, amplitudes, residual_in):
    rows, width = amplitudes.shape
    cut, kept = 1024, rows - 208
    facing = exchange(amplitudes, 1)
    high, low = align(integrals, tile_pattern)
    n = rows // 2
    pieces = [exchange(amplitudes[i : i + n], 0) for i in range(0, rows, n)]
    partner = jnp.concatenate(pieces, 0)
    most = exchange(partner[:, :cut], 1)
    rest = [exchange(partner[:kept, cut:], 1), inside(partner[kept:, cut:])]
    moved = around(partner[kept:, cut:])
    moved = jnp.pad(moved, ((48, 0), (0, 0)))
    acc = add_products(residual_in, high, low, [(OWN, 0, amplitudes), (PARTNER, 0, partner)], 256, "near", 12 * rows * rows * width)
    facing, acc, moved = lax.optimization_barrier((facing, acc, moved))
    n = rows // 2
    beside = [exchange(facing[i : i + n], 0) for i in range(0, rows, n)]
    parts = [(FACING, 0, facing), (BESIDE, 0, jnp.concatenate(beside, 0))]
    acc = add_products(acc, high, low, parts, 256, "middle", 1, [(BEYOND, 1, moved)])
    result = add_last(acc, high, low, [most], 0, None, "last0")
    return add_last(acc, high, low, rest, cut, result, "last1")


def solution(mesh):
    return jax.shard_map(
        per_device,
        mesh=mesh,
        in_specs=(P("blk", None), P("blk", None), P("blk", None), P("blk", None)),
        out_specs=P("blk", None),
        check_vma=False,
    )
```

```python
import functools

import jax
import jax.numpy as jnp
from jax import lax
from jax.experimental import pallas as pl
from jax.experimental.pallas import tpu as pltpu
from jax.sharding import PartitionSpec as P

TB = 128
W = 8
BAND = 2 * W + 1
AXIS = "blk"

OWN, PARTNER, FACING, BESIDE, BEYOND = range(5)


def exchange(value, offset):
    count = lax.axis_size(AXIS)
    pairs = []
    for low in range(offset, count + offset, 2):
        a, b = low % count, (low + 1) % count
        pairs += [(a, b), (b, a)]
    return lax.ppermute(value, AXIS, pairs)


def split(x):
    high = x.astype(jnp.bfloat16)
    low = (x - high.astype(jnp.float32)).astype(jnp.bfloat16)
    return high, low


def align_kernel(tiles, pattern_ref, v_ref, high_ref, low_ref):
    row = pl.program_id(0)
    odd = lax.rem(lax.axis_index(AXIS), 2)
    sign = 1 - 2 * odd
    for role, step in ((OWN, 0), (PARTNER, 1), (FACING, -1), (BESIDE, 2), (BEYOND, -2)):
        block = 2 + sign * step
        for t in range(tiles):
            k = block * tiles + t - row
            inside = jnp.logical_and(k >= 0, k < BAND)
            k = jnp.clip(k, 0, BAND - 1)
            keep = jnp.where(inside, pattern_ref[row, k], 0).astype(jnp.float32)
            tile = v_ref[:, pl.ds(pl.multiple_of(k * TB, TB), TB)] * keep
            high, low = split(tile)
            high_ref[role, :, t * TB : (t + 1) * TB] = high
            low_ref[role, :, t * TB : (t + 1) * TB] = low


def align(integrals, tile_pattern):
    rows = integrals.shape[0]
    tiles = rows // TB
    shape = jax.ShapeDtypeStruct((5, rows, rows), jnp.bfloat16)
    spec = pl.BlockSpec((5, TB, rows), lambda r: (0, r, 0))
    return pl.pallas_call(
        functools.partial(align_kernel, tiles),
        grid=(tiles,),
        in_specs=[
            pl.BlockSpec(memory_space=pltpu.SMEM),
            pl.BlockSpec((TB, BAND * TB), lambda r: (r, 0)),
        ],
        out_specs=[spec, spec],
        out_shape=[shape, shape],
        compiler_params=pltpu.CompilerParams(vmem_limit_bytes=24 * 2**20),
        cost_estimate=pl.CostEstimate(flops=10 * rows * rows, bytes_accessed=10**7, transcendentals=0),
        name="align",
    )(tile_pattern, integrals)


def product(vh_ref, vl_ref, t_ref):
    th, tl = split(t_ref[...])
    vh, vl = vh_ref[0], vl_ref[0]
    dot = functools.partial(jnp.dot, preferred_element_type=jnp.float32)
    return dot(vh, th) + (dot(vh, tl) + dot(vl, th))


def add_kernel(count, *refs):
    *blocks, acc_ref, out_ref = refs
    total = acc_ref[...]
    for i in range(count):
        total += product(*blocks[3 * i : 3 * i + 3])
    out_ref[...] = total
    if len(blocks) > 3 * count:

        @pl.when(pl.program_id(0) == pl.num_programs(0) - 1)
        def _():
            out_ref[...] += product(*blocks[3 * count :])


def add_products(acc, high, low, parts, cols, name, flops, edge=()):
    rows, width = acc.shape
    args, specs = [], []
    for role, piece, block in parts:
        deep = block.shape[0]
        spec = pl.BlockSpec((1, rows, deep), lambda j, role=role, piece=piece: (role, 0, piece))
        args += [high, low, block]
        specs += [spec, spec, pl.BlockSpec((deep, cols), lambda j: (0, j))]
    for role, piece, block in edge:
        deep = block.shape[0]
        spec = pl.BlockSpec((1, rows, deep), lambda j, role=role, piece=piece: (role, 0, piece))
        args += [high, low, block]
        specs += [spec, spec, pl.BlockSpec((deep, cols), lambda j: (0, 0))]
    args.append(acc)
    specs.append(pl.BlockSpec((rows, cols), lambda j: (0, j)))
    n = len(parts)
    return pl.pallas_call(
        functools.partial(add_kernel, n),
        grid=(width // cols,),
        in_specs=specs,
        out_specs=pl.BlockSpec((rows, cols), lambda j: (0, j)),
        out_shape=jax.ShapeDtypeStruct(acc.shape, acc.dtype),
        compiler_params=pltpu.CompilerParams(vmem_limit_bytes=32 * 2**20),
        cost_estimate=pl.CostEstimate(flops=flops, bytes_accessed=1, transcendentals=0),
        name=name,
    )(*args)


def joined(pieces):
    if len(pieces) == 1:
        return pieces[0]
    rest, inner, short = pieces
    cut = short.shape[0]
    return jnp.concatenate([rest, inner[:cut] + short, inner[cut:]], 0)


def last_kernel(start, step, count, *refs):
    high_ref, low_ref, acc_ref = refs[:3]
    block_refs = refs[3 : 3 + count]
    out_ref, stage, sems = refs[-3:]
    copies = []
    for i in range(stage.shape[1] // step):
        here = slice(i * step, i * step + step)
        there = slice(start + i * step, start + i * step + step)
        th, tl = split(joined([ref[:, here] for ref in block_refs]))
        vh, vl = high_ref[BEYOND], low_ref[BEYOND]
        dot = functools.partial(jnp.dot, preferred_element_type=jnp.float32)
        stage[:, here] = acc_ref[:, there] + (dot(vh, th) + (dot(vh, tl) + dot(vl, th)))
        copies.append(pltpu.make_async_copy(stage.at[:, here], out_ref.at[:, there], sems.at[i]))
        copies[-1].start()
    for copy in copies:
        copy.wait()


def add_last(acc, high, low, blocks, start, out, name):
    rows, width = acc.shape[0], blocks[0].shape[1]
    step = 256
    args = [high, low, acc, *blocks]
    specs = [pl.BlockSpec(memory_space=pltpu.VMEM)] * len(args)
    aliases = {}
    if out is not None:
        aliases = {len(args): 0}
        args.append(out)
        specs.append(pl.BlockSpec(memory_space=pl.ANY))
    return pl.pallas_call(
        functools.partial(last_kernel, start, step, len(blocks)),
        in_specs=specs,
        out_specs=pl.BlockSpec(memory_space=pl.ANY),
        out_shape=jax.ShapeDtypeStruct(acc.shape, acc.dtype),
        input_output_aliases=aliases,
        scratch_shapes=[pltpu.VMEM((rows, width), jnp.float32), pltpu.SemaphoreType.DMA((width // step,))],
        compiler_params=pltpu.CompilerParams(vmem_limit_bytes=16 * 2**20),
        cost_estimate=pl.CostEstimate(flops=1, bytes_accessed=1, transcendentals=0),
        name=name,
    )(*args)


def facing_pairs(kind):
    count = lax.axis_size(AXIS)
    pairs = [(i, (i + 1 if i % 2 else i - 1) % count) for i in range(count)]
    ends = {"inside": (1, 16), "x": (16, 64), "y": (64, count + 1)}[kind]
    border = lambda i: next(size for size in (count, 64, 16, 1) if size <= count and (i + 1) % size < 2)
    return [pair for pair in pairs if ends[0] <= border(pair[0]) < ends[1]]


def detours(one, two):
    count = lax.axis_size(AXIS)
    along, beside = [[], [], []], [[], []]
    for b in range(0, count, 16):
        for route in ((b - 1, b + 9, b + 3, b), (b, b - 10, b - 4, b - 1)):
            for hop, (i, j) in enumerate(zip(route, route[1:])):
                along[hop].append((i % count, j % count))
    for b in range(0, count, 64):
        for route in ((b - 2, b + 14, b), (b + 1, b - 15, b - 1)):
            for hop, (i, j) in enumerate(zip(route, route[1:])):
                beside[hop].append((i % count, j % count))
    for pairs in along:
        one = lax.ppermute(one, AXIS, pairs)
    for pairs in beside:
        two = lax.ppermute(two, AXIS, pairs)
    return one, two


def per_device(integrals, tile_pattern, amplitudes, residual_in):
    rows, width = amplitudes.shape
    deep = 128
    cut, first, second = 1024, rows - 2 * deep, rows - deep
    facing = exchange(amplitudes, 1)
    high, low = align(integrals, tile_pattern)
    n = rows // 2
    pieces = [exchange(amplitudes[i : i + n], 0) for i in range(0, rows, n)]
    partner = jnp.concatenate(pieces, 0)
    most = exchange(partner[:, :cut], 1)
    rest = [exchange(partner[:first, cut:], 1)]
    rest.append(lax.ppermute(partner[first:, cut:], AXIS, facing_pairs("inside")))
    rest.append(lax.ppermute(partner[first:second, cut:], AXIS, facing_pairs("x")))
    mine, partner = lax.optimization_barrier((amplitudes, partner))
    one, two = detours(partner[second:, cut:], mine[first:second, cut:])
    moved = jnp.concatenate([two, one], 0)
    acc = add_products(residual_in, high, low, [(OWN, 0, amplitudes), (PARTNER, 0, partner)], 256, "near", 6 * rows * rows * width)
    facing, acc, moved = lax.optimization_barrier((facing, acc, moved))
    n = rows // 2
    beside = [exchange(facing[i : i + n], 0) for i in range(0, rows, n)]
    parts = [(FACING, 0, facing), (BESIDE, 0, jnp.concatenate(beside, 0))]
    acc = add_products(acc, high, low, parts, 256, "middle", 1, [(BEYOND, 1, moved)])
    result = add_last(acc, high, low, [most], 0, None, "last0")
    return add_last(acc, high, low, rest, cut, result, "last1")


def solution(mesh):
    return jax.shard_map(
        per_device,
        mesh=mesh,
        in_specs=(P("blk", None), P("blk", None), P("blk", None), P("blk", None)),
        out_specs=P("blk", None),
        check_vma=False,
    )
```

```python
import functools

import jax
import jax.numpy as jnp
from jax import lax
from jax.experimental import pallas as pl
from jax.experimental.pallas import tpu as pltpu
from jax.sharding import PartitionSpec as P

TB = 128
W = 8
BAND = 2 * W + 1
AXIS = "blk"

OWN, PARTNER, FACING, BESIDE, BEYOND = range(5)


def exchange(value, offset):
    count = lax.axis_size(AXIS)
    pairs = []
    for low in range(offset, count + offset, 2):
        a, b = low % count, (low + 1) % count
        pairs += [(a, b), (b, a)]
    return lax.ppermute(value, AXIS, pairs)


def split(x):
    high = x.astype(jnp.bfloat16)
    low = (x - high.astype(jnp.float32)).astype(jnp.bfloat16)
    return high, low


def align_kernel(tiles, pattern_ref, v_ref, high_ref, low_ref):
    row = pl.program_id(0)
    odd = lax.rem(lax.axis_index(AXIS), 2)
    sign = 1 - 2 * odd
    for role, step in ((OWN, 0), (PARTNER, 1), (FACING, -1), (BESIDE, 2), (BEYOND, -2)):
        block = 2 + sign * step
        for t in range(tiles):
            k = block * tiles + t - row
            inside = jnp.logical_and(k >= 0, k < BAND)
            k = jnp.clip(k, 0, BAND - 1)
            keep = jnp.where(inside, pattern_ref[row, k], 0).astype(jnp.float32)
            tile = v_ref[:, pl.ds(pl.multiple_of(k * TB, TB), TB)] * keep
            high, low = split(tile)
            high_ref[role, :, t * TB : (t + 1) * TB] = high
            low_ref[role, :, t * TB : (t + 1) * TB] = low


def align(integrals, tile_pattern):
    rows = integrals.shape[0]
    tiles = rows // TB
    shape = jax.ShapeDtypeStruct((5, rows, rows), jnp.bfloat16)
    spec = pl.BlockSpec((5, TB, rows), lambda r: (0, r, 0))
    return pl.pallas_call(
        functools.partial(align_kernel, tiles),
        grid=(tiles,),
        in_specs=[
            pl.BlockSpec(memory_space=pltpu.SMEM),
            pl.BlockSpec((TB, BAND * TB), lambda r: (r, 0)),
        ],
        out_specs=[spec, spec],
        out_shape=[shape, shape],
        compiler_params=pltpu.CompilerParams(vmem_limit_bytes=24 * 2**20),
        cost_estimate=pl.CostEstimate(flops=10 * rows * rows, bytes_accessed=10**7, transcendentals=0),
        name="align",
    )(tile_pattern, integrals)


def product(vh_ref, vl_ref, t_ref):
    th, tl = split(t_ref[...])
    vh, vl = vh_ref[0], vl_ref[0]
    dot = functools.partial(jnp.dot, preferred_element_type=jnp.float32)
    return dot(vh, th) + (dot(vh, tl) + dot(vl, th))


def add_kernel(count, *refs):
    *blocks, acc_ref, out_ref = refs
    total = acc_ref[...]
    for i in range(count):
        total += product(*blocks[3 * i : 3 * i + 3])
    out_ref[...] = total
    if len(blocks) > 3 * count:

        @pl.when(pl.program_id(0) == pl.num_programs(0) - 1)
        def _():
            out_ref[...] += product(*blocks[3 * count :])


def add_products(acc, high, low, parts, cols, name, flops, edge=()):
    rows, width = acc.shape
    args, specs = [], []
    for role, piece, block in parts:
        deep = block.shape[0]
        spec = pl.BlockSpec((1, rows, deep), lambda j, role=role, piece=piece: (role, 0, piece))
        args += [high, low, block]
        specs += [spec, spec, pl.BlockSpec((deep, cols), lambda j: (0, j))]
    for role, piece, block in edge:
        deep = block.shape[0]
        spec = pl.BlockSpec((1, rows, deep), lambda j, role=role, piece=piece: (role, 0, piece))
        args += [high, low, block]
        specs += [spec, spec, pl.BlockSpec((deep, cols), lambda j: (0, 0))]
    args.append(acc)
    specs.append(pl.BlockSpec((rows, cols), lambda j: (0, j)))
    n = len(parts)
    return pl.pallas_call(
        functools.partial(add_kernel, n),
        grid=(width // cols,),
        in_specs=specs,
        out_specs=pl.BlockSpec((rows, cols), lambda j: (0, j)),
        out_shape=jax.ShapeDtypeStruct(acc.shape, acc.dtype),
        compiler_params=pltpu.CompilerParams(vmem_limit_bytes=32 * 2**20),
        cost_estimate=pl.CostEstimate(flops=flops, bytes_accessed=1, transcendentals=0),
        name=name,
    )(*args)


def row_halves(refs, here):
    if len(refs) == 1:
        half = refs[0].shape[0] // 2
        return refs[0][:half, here], refs[0][half:, here]
    rest, inner, short = [ref[:, here] for ref in refs]
    cut = short.shape[0]
    return rest, jnp.concatenate([inner[:cut] + short, inner[cut:]], 0)


def last_kernel(start, step, count, *refs):
    high_ref, low_ref, acc_ref = refs[:3]
    block_refs = refs[3 : 3 + count]
    out_ref, stage, sems = refs[-3:]
    half = acc_ref.shape[0] // 2
    odd = lax.rem(lax.axis_index(AXIS), 2)
    full = pl.ds(pl.multiple_of(odd * half, half), half)
    part = pl.ds(pl.multiple_of((1 - odd) * half, half), half)
    dot = functools.partial(jnp.dot, preferred_element_type=jnp.float32)
    copies = []
    for i in range(stage.shape[1] // step):
        here = slice(i * step, i * step + step)
        there = slice(start + i * step, start + i * step + step)
        upper, lower = row_halves(block_refs, here)
        th, tl = split(jnp.concatenate([upper, lower], 0))
        vh, vl = high_ref[BEYOND, full], low_ref[BEYOND, full]
        stage[full, here] = acc_ref[full, there] + (dot(vh, th) + (dot(vh, tl) + dot(vl, th)))
        th, tl = split(jnp.where(odd == 1, upper, lower))
        vh, vl = high_ref[BEYOND, part, part], low_ref[BEYOND, part, part]
        stage[part, here] = acc_ref[part, there] + (dot(vh, th) + (dot(vh, tl) + dot(vl, th)))
        copies.append(pltpu.make_async_copy(stage.at[:, here], out_ref.at[:, there], sems.at[i]))
        copies[-1].start()
    for copy in copies:
        copy.wait()


def add_last(acc, high, low, blocks, start, out, name):
    rows, width = acc.shape[0], blocks[0].shape[1]
    step = 256
    args = [high, low, acc, *blocks]
    specs = [pl.BlockSpec(memory_space=pltpu.VMEM)] * len(args)
    aliases = {}
    if out is not None:
        aliases = {len(args): 0}
        args.append(out)
        specs.append(pl.BlockSpec(memory_space=pl.ANY))
    return pl.pallas_call(
        functools.partial(last_kernel, start, step, len(blocks)),
        in_specs=specs,
        out_specs=pl.BlockSpec(memory_space=pl.ANY),
        out_shape=jax.ShapeDtypeStruct(acc.shape, acc.dtype),
        input_output_aliases=aliases,
        scratch_shapes=[pltpu.VMEM((rows, width), jnp.float32), pltpu.SemaphoreType.DMA((width // step,))],
        compiler_params=pltpu.CompilerParams(vmem_limit_bytes=16 * 2**20),
        cost_estimate=pl.CostEstimate(flops=1, bytes_accessed=1, transcendentals=0),
        name=name,
    )(*args)


def facing_pairs(kind):
    count = lax.axis_size(AXIS)
    pairs = [(i, (i + 1 if i % 2 else i - 1) % count) for i in range(count)]
    ends = {"inside": (1, 16), "x": (16, 64), "y": (64, count + 1)}[kind]
    border = lambda i: next(size for size in (count, 64, 16, 1) if size <= count and (i + 1) % size < 2)
    return [pair for pair in pairs if ends[0] <= border(pair[0]) < ends[1]]


def detours(one, two):
    count = lax.axis_size(AXIS)
    along, beside = [[], [], []], [[], []]
    for b in range(0, count, 16):
        for route in ((b - 1, b + 9, b + 3, b), (b, b - 10, b - 4, b - 1)):
            for hop, (i, j) in enumerate(zip(route, route[1:])):
                along[hop].append((i % count, j % count))
    for b in range(0, count, 64):
        for route in ((b - 2, b + 14, b), (b + 1, b - 15, b - 1)):
            for hop, (i, j) in enumerate(zip(route, route[1:])):
                beside[hop].append((i % count, j % count))
    for pairs in along:
        one = lax.ppermute(one, AXIS, pairs)
    for pairs in beside:
        two = lax.ppermute(two, AXIS, pairs)
    return one, two


def per_device(integrals, tile_pattern, amplitudes, residual_in):
    rows, width = amplitudes.shape
    cut, first, second = 1024, rows - 256, rows - 144
    facing = exchange(amplitudes, 1)
    high, low = align(integrals, tile_pattern)
    n = rows // 2
    pieces = [exchange(amplitudes[i : i + n], 0) for i in range(0, rows, n)]
    partner = jnp.concatenate(pieces, 0)
    most = exchange(partner[:, :cut], 1)
    rest = [exchange(partner[:first, cut:], 1)]
    rest.append(lax.ppermute(partner[first:, cut:], AXIS, facing_pairs("inside")))
    rest.append(lax.ppermute(partner[first:second, cut:], AXIS, facing_pairs("x")))
    mine, partner = lax.optimization_barrier((amplitudes, partner))
    one, two = detours(partner[second:, cut:], mine[first:second, cut:])
    moved = jnp.concatenate([two, one], 0)
    acc = add_products(residual_in, high, low, [(OWN, 0, amplitudes), (PARTNER, 0, partner)], 256, "near", 6 * rows * rows * width)
    facing, acc, moved = lax.optimization_barrier((facing, acc, moved))
    n = rows // 2
    beside = [exchange(facing[i : i + n], 0) for i in range(0, rows, n)]
    parts = [(FACING, 0, facing), (BESIDE, 0, jnp.concatenate(beside, 0))]
    acc = add_products(acc, high, low, parts, 256, "middle", 1, [(BEYOND, 1, moved)])
    result = add_last(acc, high, low, [most], 0, None, "last0")
    return add_last(acc, high, low, rest, cut, result, "last1")


def solution(mesh):
    return jax.shard_map(
        per_device,
        mesh=mesh,
        in_specs=(P("blk", None), P("blk", None), P("blk", None), P("blk", None)),
        out_specs=P("blk", None),
        check_vma=False,
    )
```

```python
import functools

import jax
import jax.numpy as jnp
from jax import lax
from jax.experimental import pallas as pl
from jax.experimental.pallas import tpu as pltpu
from jax.sharding import PartitionSpec as P

TB = 128
W = 8
BAND = 2 * W + 1
AXIS = "blk"

OWN, PARTNER, FACING, BESIDE, BEYOND = range(5)


def exchange(value, offset):
    count = lax.axis_size(AXIS)
    pairs = []
    for low in range(offset, count + offset, 2):
        a, b = low % count, (low + 1) % count
        pairs += [(a, b), (b, a)]
    return lax.ppermute(value, AXIS, pairs)


def split(x):
    high = x.astype(jnp.bfloat16)
    low = (x - high.astype(jnp.float32)).astype(jnp.bfloat16)
    return high, low


def align_kernel(tiles, pattern_ref, v_ref, high_ref, low_ref):
    row = pl.program_id(0)
    odd = lax.rem(lax.axis_index(AXIS), 2)
    sign = 1 - 2 * odd
    for role, step in ((OWN, 0), (PARTNER, 1), (FACING, -1), (BESIDE, 2), (BEYOND, -2)):
        block = 2 + sign * step
        for t in range(tiles):
            k = block * tiles + t - row
            inside = jnp.logical_and(k >= 0, k < BAND)
            k = jnp.clip(k, 0, BAND - 1)
            keep = jnp.where(inside, pattern_ref[row, k], 0).astype(jnp.float32)
            tile = v_ref[:, pl.ds(pl.multiple_of(k * TB, TB), TB)] * keep
            high, low = split(tile)
            high_ref[role, :, t * TB : (t + 1) * TB] = high
            low_ref[role, :, t * TB : (t + 1) * TB] = low


def align(integrals, tile_pattern):
    rows = integrals.shape[0]
    tiles = rows // TB
    shape = jax.ShapeDtypeStruct((5, rows, rows), jnp.bfloat16)
    spec = pl.BlockSpec((5, TB, rows), lambda r: (0, r, 0))
    return pl.pallas_call(
        functools.partial(align_kernel, tiles),
        grid=(tiles,),
        in_specs=[
            pl.BlockSpec(memory_space=pltpu.SMEM),
            pl.BlockSpec((TB, BAND * TB), lambda r: (r, 0)),
        ],
        out_specs=[spec, spec],
        out_shape=[shape, shape],
        compiler_params=pltpu.CompilerParams(vmem_limit_bytes=24 * 2**20),
        cost_estimate=pl.CostEstimate(flops=10 * rows * rows, bytes_accessed=10**7, transcendentals=0),
        name="align",
    )(tile_pattern, integrals)


def product(vh_ref, vl_ref, t_ref):
    th, tl = split(t_ref[...])
    vh, vl = vh_ref[0], vl_ref[0]
    dot = functools.partial(jnp.dot, preferred_element_type=jnp.float32)
    return dot(vh, th) + (dot(vh, tl) + dot(vl, th))


def add_kernel(count, *refs):
    *blocks, acc_ref, out_ref = refs
    total = acc_ref[...]
    for i in range(count):
        total += product(*blocks[3 * i : 3 * i + 3])
    out_ref[...] = total
    if len(blocks) > 3 * count:

        @pl.when(pl.program_id(0) == pl.num_programs(0) - 1)
        def _():
            out_ref[...] += product(*blocks[3 * count :])


def add_products(acc, high, low, parts, cols, name, flops, edge=()):
    rows, width = acc.shape
    args, specs = [], []
    for role, piece, block in parts:
        deep = block.shape[0]
        spec = pl.BlockSpec((1, rows, deep), lambda j, role=role, piece=piece: (role, 0, piece))
        args += [high, low, block]
        specs += [spec, spec, pl.BlockSpec((deep, cols), lambda j: (0, j))]
    for role, piece, block in edge:
        deep = block.shape[0]
        spec = pl.BlockSpec((1, rows, deep), lambda j, role=role, piece=piece: (role, 0, piece))
        args += [high, low, block]
        specs += [spec, spec, pl.BlockSpec((deep, cols), lambda j: (0, 0))]
    args.append(acc)
    specs.append(pl.BlockSpec((rows, cols), lambda j: (0, j)))
    n = len(parts)
    return pl.pallas_call(
        functools.partial(add_kernel, n),
        grid=(width // cols,),
        in_specs=specs,
        out_specs=pl.BlockSpec((rows, cols), lambda j: (0, j)),
        out_shape=jax.ShapeDtypeStruct(acc.shape, acc.dtype),
        compiler_params=pltpu.CompilerParams(vmem_limit_bytes=32 * 2**20),
        cost_estimate=pl.CostEstimate(flops=flops, bytes_accessed=1, transcendentals=0),
        name=name,
    )(*args)


def row_halves(refs, here):
    if len(refs) == 1:
        half = refs[0].shape[0] // 2
        return refs[0][:half, here], refs[0][half:, here]
    rest, inner, short = [ref[:, here] for ref in refs]
    cut = short.shape[0]
    return rest, jnp.concatenate([inner[:cut] + short, inner[cut:]], 0)


def last_kernel(start, step, count, *refs):
    high_ref, low_ref, acc_ref = refs[:3]
    block_refs = refs[3 : 3 + count]
    out_ref, stage, sems = refs[-3:]
    half = acc_ref.shape[0] // 2
    odd = lax.rem(lax.axis_index(AXIS), 2)
    full = pl.ds(pl.multiple_of(odd * half, half), half)
    part = pl.ds(pl.multiple_of((1 - odd) * half, half), half)
    dot = functools.partial(jnp.dot, preferred_element_type=jnp.float32)
    copies = []
    for i in range(stage.shape[1] // step):
        here = slice(i * step, i * step + step)
        there = slice(start + i * step, start + i * step + step)
        upper, lower = row_halves(block_refs, here)
        th, tl = split(jnp.where(odd == 1, upper, lower))
        vh, vl = high_ref[BEYOND, part, part], low_ref[BEYOND, part, part]
        stage[part, here] = acc_ref[part, there] + (dot(vh, th) + (dot(vh, tl) + dot(vl, th)))
        copies.append(pltpu.make_async_copy(stage.at[part, here], out_ref.at[part, there], sems.at[2 * i]))
        copies[-1].start()
        th, tl = split(jnp.concatenate([upper, lower], 0))
        vh, vl = high_ref[BEYOND, full], low_ref[BEYOND, full]
        stage[full, here] = acc_ref[full, there] + (dot(vh, th) + (dot(vh, tl) + dot(vl, th)))
        copies.append(pltpu.make_async_copy(stage.at[full, here], out_ref.at[full, there], sems.at[2 * i + 1]))
        copies[-1].start()
    for copy in copies:
        copy.wait()


def add_last(acc, high, low, blocks, start, out, name):
    rows, width = acc.shape[0], blocks[0].shape[1]
    step = 256
    args = [high, low, acc, *blocks]
    specs = [pl.BlockSpec(memory_space=pltpu.VMEM)] * len(args)
    aliases = {}
    if out is not None:
        aliases = {len(args): 0}
        args.append(out)
        specs.append(pl.BlockSpec(memory_space=pl.ANY))
    return pl.pallas_call(
        functools.partial(last_kernel, start, step, len(blocks)),
        in_specs=specs,
        out_specs=pl.BlockSpec(memory_space=pl.ANY),
        out_shape=jax.ShapeDtypeStruct(acc.shape, acc.dtype),
        input_output_aliases=aliases,
        scratch_shapes=[pltpu.VMEM((rows, width), jnp.float32), pltpu.SemaphoreType.DMA((2 * width // step,))],
        compiler_params=pltpu.CompilerParams(vmem_limit_bytes=16 * 2**20),
        cost_estimate=pl.CostEstimate(flops=1, bytes_accessed=1, transcendentals=0),
        name=name,
    )(*args)


def facing_pairs(kind):
    count = lax.axis_size(AXIS)
    pairs = [(i, (i + 1 if i % 2 else i - 1) % count) for i in range(count)]
    ends = {"inside": (1, 16), "x": (16, 64), "y": (64, count + 1)}[kind]
    border = lambda i: next(size for size in (count, 64, 16, 1) if size <= count and (i + 1) % size < 2)
    return [pair for pair in pairs if ends[0] <= border(pair[0]) < ends[1]]


def detours(one, two):
    count = lax.axis_size(AXIS)
    along, beside = [[], [], []], [[], []]
    for b in range(0, count, 16):
        for route in ((b - 1, b + 9, b + 3, b), (b, b - 10, b - 4, b - 1)):
            for hop, (i, j) in enumerate(zip(route, route[1:])):
                along[hop].append((i % count, j % count))
    for b in range(0, count, 64):
        for route in ((b - 2, b + 14, b), (b + 1, b - 15, b - 1)):
            for hop, (i, j) in enumerate(zip(route, route[1:])):
                beside[hop].append((i % count, j % count))
    for pairs in along:
        one = lax.ppermute(one, AXIS, pairs)
    for pairs in beside:
        two = lax.ppermute(two, AXIS, pairs)
    return one, two


def per_device(integrals, tile_pattern, amplitudes, residual_in):
    rows, width = amplitudes.shape
    cut, first, second = 1024, rows - 256, rows - 144
    facing = exchange(amplitudes, 1)
    high, low = align(integrals, tile_pattern)
    n = rows // 2
    pieces = [exchange(amplitudes[i : i + n], 0) for i in range(0, rows, n)]
    partner = jnp.concatenate(pieces, 0)
    most = exchange(partner[:, :cut], 1)
    rest = [exchange(partner[:first, cut:], 1)]
    rest.append(lax.ppermute(partner[first:, cut:], AXIS, facing_pairs("inside")))
    rest.append(lax.ppermute(partner[first:second, cut:], AXIS, facing_pairs("x")))
    mine, partner = lax.optimization_barrier((amplitudes, partner))
    one, two = detours(partner[second:, cut:], mine[first:second, cut:])
    moved = jnp.concatenate([two, one], 0)
    acc = add_products(residual_in, high, low, [(OWN, 0, amplitudes), (PARTNER, 0, partner)], 256, "near", 6 * rows * rows * width)
    facing, acc, moved = lax.optimization_barrier((facing, acc, moved))
    n = rows // 2
    beside = [exchange(facing[i : i + n], 0) for i in range(0, rows, n)]
    parts = [(FACING, 0, facing), (BESIDE, 0, jnp.concatenate(beside, 0))]
    acc = add_products(acc, high, low, parts, 256, "middle", 1, [(BEYOND, 1, moved)])
    result = add_last(acc, high, low, [most], 0, None, "last0")
    return add_last(acc, high, low, rest, cut, result, "last1")


def solution(mesh):
    return jax.shard_map(
        per_device,
        mesh=mesh,
        in_specs=(P("blk", None), P("blk", None), P("blk", None), P("blk", None)),
        out_specs=P("blk", None),
        check_vma=False,
    )
```
